256 devices in a mesh: req: 128 (over z, y, x), tp: 2 (over core).
Axes of the slice: x: 4, y: 4, z: 8, core: 2. Of those that a mesh axis runs over, the one named last changes fastest.
Arguments:
- stretch_states: bfloat16 [128, 128, 8192], P('req', None, 'tp'), may hold values from -6 to 6
- w_down: bfloat16 [8192, 512], P('tp'), may hold values from -0.0625 to 0.0625
- latent_gain: float32 [512], replicated, may hold values from 0.5 to 1.5
- queries: bfloat16 [128, 128, 64, 512], P('req', None, 'tp'), may hold values from -40 to 40
- page_pool: bfloat16 [128, 128, 16, 512], P('req', None, 'tp'), may hold values from -4 to 4, as said below
- page_table: int32 [128, 128], P('req'), may hold values from 0 to 127, as said below
- prefix_len: int32 [128], P('req'), may hold values from 16 to 2048, as said below
Outputs:
- new_latents: bfloat16 [128, 128, 512], P('req', 'tp')
- attended: bfloat16 [128, 128, 64, 512], P('req', None, 'tp')
The draws below stay inside these ranges and needn't reach their ends.
Inputs may be any that keep to these rules, and one draw needn't show every extreme that they name: `prefix_len`: some request has exactly 2048 cached tokens and some exactly 16. Each row is a permutation of the devices: logical page j of request r is held by device page_table[r, j], in that device's slot r. `page_pool`: slot r of device d holds the latents of the page of request r that page_table names d.
All inputs are finite; a program needn't handle non-finite values.
Results may differ from the reference program's by a relative error of at most 0.004.
Values may be sent and summed in bfloat16 or wider, within the bound.
No kernel may reach another device: no remote copies, remote signals or barrier semaphores. Data moves between devices by JAX's collectives and lax.ppermute only.
A program may use at most 128 MiB of HBM per device.

```python
import jax
import jax.numpy as jnp
from jax import lax

D = 8192
HEADS = 64
LAT = 512
STRETCH = 128
PAGE_ROWS = 16
REQS = 128
PAGES = 128
PMAX = 2048
KB = 128


def layout(key):
    key_len, key_high, key_floor, key_table = jax.random.split(key, 4)
    lengths = jax.random.randint(key_len, (REQS,), PAGE_ROWS, PMAX + 1)
    longest = jax.random.randint(key_high, (), 0, REQS)
    shortest = (longest + 1 + jax.random.randint(key_floor, (), 0, REQS - 1)) % REQS
    lengths = lengths.at[longest].set(PMAX).at[shortest].set(PAGE_ROWS)
    ranks = jax.random.randint(key_table, (REQS, PAGES), 0, 1 << 20) * PAGES + jnp.arange(PAGES)[None, :]
    tables = jnp.argsort(ranks, axis=1, stable=True).astype(jnp.int32)
    return (lengths.astype(jnp.int32), tables)


def cached_rows(key):
    lengths, tables = layout(key)
    inner = jax.random.fold_in(key, 11)
    key_norm = jax.random.fold_in(inner, 0)
    key_anchor = jax.random.fold_in(inner, 2)
    normal_part = jnp.clip(jax.random.normal(key_norm, (REQS, PMAX, LAT), jnp.float32), -4.0, 4.0)
    base = normal_part
    anchor = jax.random.randint(key_anchor, (REQS,), 0, lengths - 1)
    request_ids = jnp.arange(REQS)
    row_first = base[request_ids, anchor]
    row_second = base[request_ids, anchor + 1]
    coord = jnp.arange(LAT)
    upper = coord >= LAT // 2
    row_second = jnp.where(upper[None, :], row_second, row_first)
    row_first = jnp.where((coord == LAT // 2)[None, :], 1.5, row_first)
    row_second = jnp.where((coord == LAT // 2)[None, :], 0.0, row_second)
    base = base.at[request_ids, anchor].set(row_first).at[request_ids, anchor + 1].set(row_second)
    return (tables, base)


def draw_prefix_len(key, part):
    lengths, tables = layout(key)
    return lengths


def draw_page_table(key, part):
    lengths, tables = layout(key)
    return tables


def draw_page_pool(key, part):
    tables, base = cached_rows(key)
    logical = base.reshape(REQS, PAGES, PAGE_ROWS, LAT)
    slots = jnp.broadcast_to(jnp.arange(REQS)[:, None], (REQS, PAGES))
    pool = jnp.zeros((REQS, REQS, PAGE_ROWS, LAT), jnp.float32).at[tables, slots].set(logical)
    return pool.astype(jnp.bfloat16)


def draw_queries(key, part):
    inner = jax.random.fold_in(key, 5)
    key_norm = jax.random.fold_in(inner, 0)
    shape = (REQS, STRETCH, HEADS, LAT)
    normal_part = jnp.clip(jax.random.normal(key_norm, shape, jnp.float32), -4.0, 4.0)
    drawn = normal_part
    mixed = drawn.at[:, :4].set(drawn[:, :4])
    return mixed.astype(jnp.bfloat16)


def steps_of(rng, extent, pieces, smallest, top_value):
    factor_of = 1.0
    for position, blocks in pieces:
        heights = jax.random.uniform(jax.random.fold_in(jax.random.fold_in(rng, 6), position), (blocks,), jnp.float32, smallest / len(pieces), top_value / len(pieces))
        factor_of = factor_of * jnp.repeat(jnp.exp(heights), extent[position] // blocks).reshape((-1,) + (1,) * (len(extent) - 1 - position))
    return factor_of


def normal_values(key, dims, width, bound, cuts=(), held_as=jnp.bfloat16):
    result = jax.random.normal(key, dims, jnp.float32) * width
    if len(cuts) > 0:
        result = steps_of(key, dims, cuts, -0.22, 0.18) * result
    return jnp.clip(result, min=-bound, max=bound).astype(held_as)


def setup_inputs(seed: int = 0) -> dict:
    key_of = jax.random.split(jax.random.key(seed), 8)
    stretch_states = normal_values(key_of[0], (REQS, STRETCH, D), 1.0, 6.0, ((0, 128), (2, 2)))
    w_down = normal_values(key_of[1], (D, LAT), D ** -0.5, 0.0625, ((0, 2),))
    latent_gain = jnp.clip(1.0 + 0.1 * jax.random.normal(key_of[2], (LAT,), jnp.float32), 0.5, 1.5)
    queries = draw_queries(jax.random.fold_in(key_of[7], 71), 0)
    page_pool = draw_page_pool(jax.random.fold_in(key_of[7], 71), 0)
    page_table = draw_page_table(jax.random.fold_in(key_of[7], 71), 0)
    prefix_len = draw_prefix_len(jax.random.fold_in(key_of[7], 71), 0)
    return dict(stretch_states=stretch_states, w_down=w_down, latent_gain=latent_gain, queries=queries, page_pool=page_pool, page_table=page_table, prefix_len=prefix_len)


SCORE_SCALE = 0.08838834764831845
MASKED = -1e+30

def normalize(summed, latent_gain):
    mean_square = lax.optimization_barrier(jnp.mean(summed * summed, axis=-1, keepdims=True))
    return (summed * lax.rsqrt(mean_square + 1e-06) * latent_gain.astype(jnp.float32)).astype(jnp.bfloat16)

def block_terms(flat_q, key_rows, visible):
    scores = jnp.dot(flat_q, key_rows.T, preferred_element_type=jnp.float32) * SCORE_SCALE
    scores = jnp.where(visible, scores, MASKED)
    highest = lax.optimization_barrier(jnp.max(scores, axis=1))
    weights = jnp.where(visible, jnp.exp(scores - highest[:, None]), 0.0)
    totals = lax.optimization_barrier(jnp.sum(weights, axis=1))
    accumulated = jnp.dot(weights.astype(jnp.bfloat16), key_rows, preferred_element_type=jnp.float32)
    return (highest, totals, accumulated)

def combine(first_terms, second_terms):
    highest = jnp.maximum(first_terms[0], second_terms[0])
    scale_first = jnp.exp(first_terms[0] - highest)
    scale_second = jnp.exp(second_terms[0] - highest)
    totals = first_terms[1] * scale_first + second_terms[1] * scale_second
    accumulated = first_terms[2] * scale_first[:, None] + second_terms[2] * scale_second[:, None]
    return (highest, totals, accumulated)

def reference(stretch_states, w_down, latent_gain, queries, page_pool, page_table, prefix_len):

    def one_request(request):
        summed = jnp.dot(stretch_states[request], w_down, preferred_element_type=jnp.float32)
        latents = normalize(summed, latent_gain)
        fetched = page_pool[page_table[request], request]
        prefix = fetched.reshape(PMAX, LAT)
        flat_q = queries[request].reshape(STRETCH * HEADS, LAT)
        query_pos = jnp.arange(STRETCH * HEADS, dtype=jnp.int32) // HEADS
        causal = jnp.arange(STRETCH, dtype=jnp.int32)[None, :] <= query_pos[:, None]
        carried = block_terms(flat_q, latents, causal)
        length = prefix_len[request]

        def advance(carried, block):
            start = (block * KB).astype(jnp.int32)
            key_rows = lax.dynamic_slice_in_dim(prefix, start, KB, 0)
            visible = (start + jnp.arange(KB, dtype=jnp.int32))[None, :] < length
            merged = combine(carried, block_terms(flat_q, key_rows, visible))
            live = start < length
            updated = tuple((jnp.where(live, fresh, previous) for fresh, previous in zip(merged, carried)))
            return (updated, None)
        carried, unused = lax.scan(advance, carried, jnp.arange(PMAX // KB, dtype=jnp.int32))
        attended = (carried[2] / carried[1][:, None]).astype(jnp.bfloat16)
        return (latents, attended.reshape(STRETCH, HEADS, LAT))
    new_latents, attended = lax.map(one_request, jnp.arange(REQS, dtype=jnp.int32))
    return (new_latents, attended)
```

```python
import functools

import jax
import jax.numpy as jnp
from jax import lax
from jax.experimental import pallas as pl
from jax.experimental.pallas import tpu as pltpu
from jax.sharding import PartitionSpec as P

SCORE_SCALE = 0.08838834764831845
LOG2_E = 1.4426950408889634
EXPONENT_SCALE = SCORE_SCALE * LOG2_E
MASKED = -1e30
VMEM_BYTES = 56 * 2**20


def normalize(summed, latent_gain):
    mean_square = jnp.mean(summed * summed, axis=-1, keepdims=True)
    return (summed * lax.rsqrt(mean_square + 1e-06) * latent_gain).astype(jnp.bfloat16)


def attention_kernel(q_ref, k_ref, bias_ref, out_ref, *, heads, new_rows, rows, parts):
    first_row = pl.program_id(0) * (rows * parts)

    def scores_of(part):
        q = q_ref[pl.ds(part * rows, rows), :]
        scores = lax.dot_general(
            q, k_ref[...], (((1,), (1,)), ((), ())), preferred_element_type=jnp.float32
        )
        row = first_row + part * rows + lax.broadcasted_iota(jnp.int32, (rows, new_rows), 0)
        key = lax.broadcasted_iota(jnp.int32, (rows, new_rows), 1)
        fresh = jnp.where(key * heads <= row, scores[:, :new_rows], MASKED)
        cached = scores[:, new_rows:] + bias_ref[...]
        return jnp.concatenate([fresh, cached], axis=1)

    def weights_of(scores):
        highest = jnp.max(scores, axis=1, keepdims=True)
        weights = jnp.exp2((scores - highest) * EXPONENT_SCALE)
        return weights.astype(jnp.bfloat16), jnp.sum(weights, axis=1, keepdims=True)

    def finish(part, weights, totals):
        accumulated = jnp.dot(weights, k_ref[...], preferred_element_type=jnp.float32)
        out_ref[pl.ds(part * rows, rows), :] = (accumulated / totals).astype(jnp.bfloat16)

    scores = scores_of(0)
    pending = None
    for part in range(parts):
        following = scores_of(part + 1) if part + 1 < parts else None
        weights, totals = weights_of(scores)
        if pending is not None:
            finish(*pending)
        pending = (part, weights, totals)
        scores = following
    finish(*pending)


def attend(flat_q, keys, bias, heads, new_rows, rows=512, parts=2):
    total_rows, width = flat_q.shape
    key_count = keys.shape[0]
    return pl.pallas_call(
        functools.partial(
            attention_kernel, heads=heads, new_rows=new_rows, rows=rows, parts=parts
        ),
        grid=(total_rows // (rows * parts),),
        in_specs=[
            pl.BlockSpec((rows * parts, width), lambda i: (i, 0)),
            pl.BlockSpec((key_count, width), lambda i: (0, 0)),
            pl.BlockSpec((1, key_count - new_rows), lambda i: (0, 0)),
        ],
        out_specs=pl.BlockSpec((rows * parts, width), lambda i: (i, 0)),
        out_shape=jax.ShapeDtypeStruct(flat_q.shape, jnp.bfloat16),
        compiler_params=pltpu.CompilerParams(vmem_limit_bytes=VMEM_BYTES),
        cost_estimate=pl.CostEstimate(
            flops=4 * total_rows * key_count * width,
            bytes_accessed=4 * total_rows * width + 2 * key_count * width,
            transcendentals=total_rows * key_count,
        ),
        name="attend",
    )(flat_q, keys, bias)


def body(stretch_states, w_down, latent_gain, queries, page_pool, page_table, prefix_len):
    swap = [(0, 1), (1, 0)]
    side = lax.axis_index("tp")
    own_pages = lax.all_to_all(page_pool[0], "req", split_axis=0, concat_axis=0, tiled=True)
    other_pages = lax.ppermute(own_pages, "tp", swap)
    partial_value = jnp.dot(stretch_states[0], w_down, preferred_element_type=jnp.float32)
    summed = partial_value + lax.ppermute(partial_value, "tp", swap)
    latents = normalize(summed, latent_gain)
    new_rows, width = latents.shape
    row_share = new_rows // 2
    own_rows = lax.dynamic_slice_in_dim(latents, side * row_share, row_share, 0)

    pages, half_rows, _ = own_pages.shape
    place = jnp.arange(pages, dtype=jnp.int32)
    logical = jnp.sum(
        jnp.where(page_table[0][None, :] == place[:, None], place[None, :], 0), axis=1
    )
    token = logical[:, None] * (2 * half_rows) + jnp.arange(half_rows, dtype=jnp.int32)[None, :]
    token = jnp.concatenate(
        [(token + side * half_rows).reshape(-1), (token + (1 - side) * half_rows).reshape(-1)]
    )
    bias = jnp.where(token < prefix_len[0], 0.0, MASKED).astype(jnp.float32)[None, :]

    keys = jnp.concatenate(
        [latents, own_pages.reshape(-1, width), other_pages.reshape(-1, width)], axis=0
    )
    heads = queries.shape[2]
    flat_q = queries[0].reshape(new_rows * heads, width)
    attended = attend(flat_q, keys, bias, heads, new_rows)
    return (own_rows[None], attended.reshape(1, new_rows, heads, width))


def solution(mesh):
    return jax.shard_map(
        body,
        mesh=mesh,
        in_specs=(
            P("req", None, "tp"),
            P("tp", None),
            P(),
            P("req", None, "tp", None),
            P("req", None, "tp", None),
            P("req", None),
            P("req"),
        ),
        out_specs=(P("req", "tp", None), P("req", None, "tp", None)),
        check_vma=False,
    )
```

```python
import functools

import jax
import jax.numpy as jnp
from jax import lax
from jax.experimental import pallas as pl
from jax.experimental.pallas import tpu as pltpu
from jax.sharding import PartitionSpec as P

SCORE_SCALE = 0.08838834764831845
LOG2_E = 1.4426950408889634
EXPONENT_SCALE = SCORE_SCALE * LOG2_E
MASKED = -1e30
LANES = 128
VMEM_BYTES = 26 * 2**20
SWAP = [(0, 1), (1, 0)]
ROWS = 512
FIRST_PARTS, NEXT_PARTS, LAST_PARTS = 2, 4, 2
RING = 8
PLANE = 16
STEPS = (0, 4, 1, 2, 3, -1, -2, -3)
FORWARD = {step: STEPS.index(step) for step in (1, 2, 3)}
BLOCKS = (
    (0, 0),
    *((0, 1), (1, 0), (1, 1), (-1, 1), (-1, 0)),
    *((2, 0), (2, 1), (-2, 1), (-2, 0)),
    *((3, 0), (3, 1), (4, 0), (-3, 1), (-3, 0), (4, 1)),
)
PHASES = ((0, 1), (1, 6), (6, 10), (10, 16))


def normalize(summed, latent_gain):
    mean_square = jnp.mean(summed * summed, axis=-1, keepdims=True)
    return (summed * lax.rsqrt(mean_square + 1e-06) * latent_gain).astype(jnp.bfloat16)


def product(first, second, contract):
    return lax.dot_general(
        first, second, (((1,), (contract,)), ((), ())), preferred_element_type=jnp.float32
    )


def across(column, count):
    return jnp.concatenate([column] * count, axis=1) if count > 1 else column


def lane_sums(weights):
    total = weights[:, :LANES]
    for start in range(LANES, weights.shape[1], LANES):
        total = total + weights[:, start : start + LANES]
    return total


def fill_keys(refs, takes, k_ref):
    @pl.when(pl.program_id(0) == 0)
    def _():
        start = 0
        for ref, (low, high) in zip(refs, takes):
            k_ref[pl.ds(start, high - low), :] = ref[pl.ds(low, high - low), :]
            start += high - low


def pipelined(parts, scores_of, weights_of, finish):
    scores = scores_of(0)
    pending = None
    for part in range(parts):
        following = scores_of(part + 1) if part + 1 < parts else None
        weighed = weights_of(part, scores)
        if pending is not None:
            finish(*pending)
        pending = (part, *weighed)
        scores = following
    finish(*pending)


def tile_rows(part):
    return pl.ds(part * ROWS, ROWS)


def all_rows(part, parts):
    return pl.ds(pl.multiple_of((pl.program_id(0) * parts + part) * ROWS, ROWS), ROWS)


def row_highest(scores):
    return jnp.broadcast_to(jnp.max(scores, axis=1, keepdims=True), (ROWS, LANES))


def weigh(scores, highest):
    return jnp.exp2((scores - across(highest, scores.shape[1] // LANES)) * EXPONENT_SCALE)


def first_kernel(q_ref, bias_ref, *refs, takes, parts, heads, new_rows, span):
    *key_refs, acc_ref, high_ref, sum_ref, held_ref, own_ref, mark_ref, k_ref = refs
    all_of = functools.partial(all_rows, parts=parts)
    fill_keys(key_refs, takes, k_ref)
    share = own_ref.shape[0]
    first_own = pl.multiple_of(lax.axis_index("tp") * share, share)
    own_ref[...] = key_refs[0][pl.ds(first_own, share), :]
    mark_ref[...] = jnp.zeros_like(mark_ref)

    def scores_of(part):
        q = q_ref[tile_rows(part), :]
        held_ref[all_of(part), :] = q
        scores = product(q, k_ref[...], 1)
        first_row = (pl.program_id(0) * parts + part) * ROWS
        row = first_row + lax.broadcasted_iota(jnp.int32, (ROWS, new_rows), 0)
        key = lax.broadcasted_iota(jnp.int32, (ROWS, new_rows), 1)
        fresh = jnp.where(key * heads <= row, scores[:, :new_rows], MASKED)
        return jnp.concatenate([fresh, scores[:, new_rows:] + bias_ref[:, slice(*span)]], axis=1)

    def weights_of(part, scores):
        highest = row_highest(scores)
        weights = weigh(scores, highest)
        high_ref[all_of(part), :] = highest
        sum_ref[all_of(part), :] = lane_sums(weights)
        return (weights.astype(jnp.bfloat16),)

    def finish(part, weights):
        acc_ref[all_of(part), :] = product(weights, k_ref[...], 0)

    pipelined(parts, scores_of, weights_of, finish)


def next_kernel(held_ref, bias_ref, acc_in, high_in, sum_in, *refs, takes, parts, span, last, marks):
    all_of = functools.partial(all_rows, parts=parts)
    refs = refs[marks:]
    if last:
        *key_refs, out_ref, k_ref = refs
    else:
        *key_refs, acc_ref, high_ref, sum_ref, mark_ref, k_ref = refs
        mark_ref[...] = jnp.zeros_like(mark_ref)
    fill_keys(key_refs, takes, k_ref)
    wide = k_ref.shape[1] // LANES

    def scores_of(part):
        scores = product(held_ref[all_of(part), :], k_ref[...], 1)
        return scores + bias_ref[:, slice(*span)]

    def weights_of(part, scores):
        before = high_in[all_of(part), :]
        highest = jnp.maximum(before, row_highest(scores))
        kept = jnp.exp2((before - highest) * EXPONENT_SCALE)
        weights = weigh(scores, highest)
        totals = sum_in[all_of(part), :] * kept + lane_sums(weights)
        if last:
            totals = jnp.broadcast_to(jnp.sum(totals, axis=1, keepdims=True), (ROWS, LANES))
        else:
            high_ref[all_of(part), :] = highest
            sum_ref[all_of(part), :] = totals
        return weights.astype(jnp.bfloat16), kept, totals

    def finish(part, weights, kept, totals):
        accumulated = acc_in[all_of(part), :] * across(kept, wide)
        accumulated = accumulated + product(weights, k_ref[...], 0)
        if last:
            share = across(1.0 / totals, wide)
            out_ref[tile_rows(part), :] = (accumulated * share).astype(jnp.bfloat16)
        else:
            acc_ref[all_of(part), :] = accumulated

    pipelined(parts, scores_of, weights_of, finish)


def sort_kernel(pool_ref, out_ref, sems):
    height = lax.axis_index("req") // PLANE
    sign = 1 - 2 * lax.axis_index("tp")
    moves = []
    for number, step in enumerate(STEPS):
        source = pool_ref.at[lax.rem(height + sign * step + RING, RING)]
        moves.append(pltpu.make_async_copy(source, out_ref.at[:, number], sems.at[number]))
    for move in moves:
        move.start()
    for move in moves:
        move.wait()


def whole(array):
    return pl.BlockSpec(array.shape, lambda i: (0,) * array.ndim)


def resident(array):
    return pltpu.with_memory_space_constraint(array, pltpu.VMEM)


RESIDENT = pl.BlockSpec(memory_space=pltpu.VMEM)


def sort_pages(pool):
    ring, plane, half_rows, width = pool.shape
    return pl.pallas_call(
        sort_kernel,
        in_specs=[pl.BlockSpec(memory_space=pl.ANY)],
        out_specs=RESIDENT,
        out_shape=pltpu.VMEM((plane, ring, half_rows, width), pool.dtype),
        scratch_shapes=[pltpu.SemaphoreType.DMA((ring,))],
        compiler_params=pltpu.CompilerParams(vmem_limit_bytes=VMEM_BYTES),
        name="sort_pages",
    )(pltpu.with_memory_space_constraint(pool, pltpu.HBM))


def attend(kernel, flat_q, keys, bias, state, mark, parts, out_specs, out_shape, aliases):
    rows, width = flat_q.shape
    takes = [(key[1:] if isinstance(key, tuple) else (0, key.shape[0])) for key in keys]
    keys = [key[0] if isinstance(key, tuple) else key for key in keys]
    key_count = sum(high - low for low, high in takes)
    q_spec = RESIDENT if state else row_tile(parts, width)
    q_space = pltpu.VMEM if state else pltpu.HBM
    return pl.pallas_call(
        functools.partial(kernel, takes=takes, parts=parts),
        grid=(rows // (ROWS * parts),),
        in_specs=[q_spec, whole(bias)]
        + [RESIDENT for _ in state]
        + [whole(part) for part in mark]
        + [RESIDENT for _ in keys],
        out_specs=out_specs,
        out_shape=out_shape,
        input_output_aliases=aliases,
        scratch_shapes=[pltpu.VMEM((key_count, width), jnp.bfloat16)],
        compiler_params=pltpu.CompilerParams(vmem_limit_bytes=VMEM_BYTES),
        cost_estimate=pl.CostEstimate(flops=0, bytes_accessed=1 << 16, transcendentals=0),
        name="attend",
    )(
        pltpu.with_memory_space_constraint(flat_q, q_space),
        bias,
        *[resident(part) for part in state],
        *mark,
        *[resident(key) for key in keys],
    )


def row_tile(parts, width):
    return pl.BlockSpec((ROWS * parts, width), lambda i: (i, 0))


def state_shapes(rows, width):
    shapes = [(rows, width), (rows, LANES), (rows, LANES)]
    return [pltpu.VMEM(shape, jnp.float32) for shape in shapes]


def attend_first(flat_q, keys, bias, span, heads):
    rows, width = flat_q.shape
    new_rows = keys[0].shape[0]
    small = [(new_rows // 2, width), (8, LANES)]
    return attend(
        functools.partial(first_kernel, heads=heads, new_rows=new_rows, span=span),
        flat_q,
        keys,
        bias,
        [],
        [],
        FIRST_PARTS,
        [RESIDENT] * 4 + [pl.BlockSpec(shape, lambda i: (0, 0)) for shape in small],
        state_shapes(rows, width)
        + [
            pltpu.VMEM((rows, width), jnp.bfloat16),
            jax.ShapeDtypeStruct(small[0], jnp.bfloat16),
            jax.ShapeDtypeStruct(small[1], jnp.float32),
        ],
        {},
    )


def attend_next(held, keys, bias, span, state, mark, last):
    rows, width = held.shape
    kernel = functools.partial(next_kernel, span=span, last=last, marks=len(mark))
    if last:
        out = row_tile(LAST_PARTS, width), jax.ShapeDtypeStruct((rows, width), jnp.bfloat16)
        return attend(kernel, held, keys, bias, state, mark, LAST_PARTS, *out, {})
    specs = [RESIDENT] * 3 + [pl.BlockSpec((8, LANES), lambda i: (0, 0))]
    shapes = state_shapes(rows, width) + [jax.ShapeDtypeStruct((8, LANES), jnp.float32)]
    aliases = {2: 0, 3: 1, 4: 2}
    return attend(kernel, held, keys, bias, state, mark, NEXT_PARTS, specs, shapes, aliases)


def along_ring(blocks, step):
    pairs = []
    for z in range(RING):
        for place in range(PLANE):
            for core, distance in ((0, step), (1, -step)):
                target = ((z + distance) % RING) * PLANE + place
                pairs.append(((z * PLANE + place) * 2 + core, target * 2 + core))
    return lax.ppermute(blocks, ("req", "tp"), pairs)


def body(stretch_states, w_down, latent_gain, queries, page_pool, page_table, prefix_len):
    side = lax.axis_index("tp")
    sign = 1 - 2 * side
    height = lax.axis_index("req") // PLANE
    half_rows, width = page_pool.shape[2:]
    pool = page_pool[0].reshape(RING, PLANE, half_rows, width)

    by_place = sort_pages(pool)
    by_place, page_table, stretch_states = lax.optimization_barrier(
        (by_place, page_table, stretch_states)
    )
    planes = [[z * PLANE + place for place in range(PLANE)] for z in range(RING)]
    crossed = lax.all_to_all(
        by_place, "req", split_axis=0, concat_axis=0, axis_index_groups=planes, tiled=True
    )
    partial_value = jnp.dot(stretch_states[0], w_down, preferred_element_type=jnp.float32)
    summed = partial_value + lax.ppermute(partial_value, "tp", SWAP)
    latents = normalize(summed, latent_gain)
    new_rows = latents.shape[0]

    place = jnp.arange(RING * PLANE, dtype=jnp.int32)
    logical = jnp.sum(
        jnp.where(page_table[0][None, :] == place[:, None], place[None, :], 0), axis=1
    ).reshape(RING, PLANE)
    steps = jnp.array([step for step, _ in BLOCKS], dtype=jnp.int32)
    others = jnp.array([other for _, other in BLOCKS], dtype=jnp.int32)
    page = jnp.take(logical, (height - sign * steps) % RING, axis=0)
    half = (side + others) % 2
    token = page[:, :, None] * (2 * half_rows) + (half * half_rows)[:, None, None]
    token = token + jnp.arange(half_rows, dtype=jnp.int32)
    bias = jnp.where(token.reshape(1, -1) < prefix_len[0], 0.0, MASKED).astype(jnp.float32)

    crossed, latents, bias = lax.optimization_barrier((crossed, latents, bias))
    handed = lax.ppermute(
        jnp.stack([crossed[:, 5], crossed[:, 6], crossed[:, 7], crossed[:, 0]]), "tp", SWAP
    )
    heads = queries.shape[2]
    flat_q = queries[0].reshape(new_rows * heads, width)
    span = lambda phase: tuple(edge * PLANE * half_rows for edge in PHASES[phase])
    block_rows = PLANE * half_rows
    flat = lambda block: block.reshape(-1, width)
    both = lambda block: [flat(block), flat(lax.ppermute(block, "tp", SWAP))]

    one = along_ring(jnp.stack([crossed[:, FORWARD[1]], handed[0], crossed[:, 1]]), 1)
    two = along_ring(jnp.stack([crossed[:, FORWARD[2]], handed[1]]), 2)
    keys = [latents, flat(crossed[:, 0])]
    *state, held, own_rows, mark = attend_first(flat_q, keys, bias, span(0), heads)

    one, mark = lax.optimization_barrier((one, mark))
    three = along_ring(jnp.stack([crossed[:, FORWARD[3]], handed[2], one[2]]), 3)
    keys = [(flat(handed), 3 * block_rows, 4 * block_rows)]
    keys += [(key, 0, 2 * block_rows) for key in both(one)]
    *state, mark = attend_next(held, keys, bias, span(1), state, [mark], False)
    two, mark = lax.optimization_barrier((two, mark))
    *state, mark = attend_next(held, both(two), bias, span(2), state, [mark], False)
    three, mark = lax.optimization_barrier((three, mark))
    attended = attend_next(held, both(three), bias, span(3), state, [mark], True)
    return (own_rows[None], attended.reshape(1, new_rows, heads, width))


def solution(mesh):
    return jax.shard_map(
        body,
        mesh=mesh,
        in_specs=(
            P("req", None, "tp"),
            P("tp", None),
            P(),
            P("req", None, "tp", None),
            P("req", None, "tp", None),
            P("req", None),
            P("req"),
        ),
        out_specs=(P("req", "tp", None), P("req", None, "tp", None)),
        check_vma=False,
    )
```

```python
import functools

import jax
import jax.numpy as jnp
from jax import lax
from jax.experimental import pallas as pl
from jax.experimental.pallas import tpu as pltpu
from jax.sharding import PartitionSpec as P

SCORE_SCALE = 0.08838834764831845
LOG2_E = 1.4426950408889634
EXPONENT_SCALE = SCORE_SCALE * LOG2_E
MASKED = -1e30
LANES = 128
VMEM_BYTES = 30 * 2**20
SWAP = [(0, 1), (1, 0)]
ROWS = 512
FIRST_PARTS, NEXT_PARTS, LAST_PARTS = 4, 4, 2
RING = 8
PLANE = 16
STEPS = (0, 4, 1, 2, 3, -1, -2, -3)
FORWARD = {step: STEPS.index(step) for step in (1, 2, 3)}
BLOCKS = (
    (0, 0),
    *((0, 1), (1, 0), (1, 1), (-1, 1), (-1, 0)),
    *((2, 0), (2, 1), (-2, 1), (-2, 0)),
    *((3, 0), (3, 1), (4, 0), (-3, 1), (-3, 0), (4, 1)),
)
PHASES = ((0, 2), (2, 6), (6, 10), (10, 16))


def normalize(summed, latent_gain):
    mean_square = jnp.mean(summed * summed, axis=-1, keepdims=True)
    return (summed * lax.rsqrt(mean_square + 1e-06) * latent_gain).astype(jnp.bfloat16)


def product(first, second, contract):
    return lax.dot_general(
        first, second, (((1,), (contract,)), ((), ())), preferred_element_type=jnp.float32
    )


def across(column, count):
    return jnp.concatenate([column] * count, axis=1) if count > 1 else column


def lane_sums(weights):
    total = weights[:, :LANES]
    for start in range(LANES, weights.shape[1], LANES):
        total = total + weights[:, start : start + LANES]
    return total


def fill_keys(refs, takes, k_ref):
    @pl.when(pl.program_id(0) == 0)
    def _():
        start = 0
        for ref, (low, high) in zip(refs, takes):
            k_ref[pl.ds(start, high - low), :] = ref[pl.ds(low, high - low), :]
            start += high - low


def pipelined(parts, scores_of, weights_of, finish):
    scores = scores_of(0)
    pending = None
    for part in range(parts):
        following = scores_of(part + 1) if part + 1 < parts else None
        weighed = weights_of(part, scores)
        if pending is not None:
            finish(*pending)
        pending = (part, *weighed)
        scores = following
    finish(*pending)


def tile_rows(part):
    return pl.ds(part * ROWS, ROWS)


def all_rows(part, parts):
    return pl.ds(pl.multiple_of((pl.program_id(0) * parts + part) * ROWS, ROWS), ROWS)


def row_highest(scores):
    return jnp.broadcast_to(jnp.max(scores, axis=1, keepdims=True), (ROWS, LANES))


def weigh(scores, highest):
    return jnp.exp2((scores - across(highest, scores.shape[1] // LANES)) * EXPONENT_SCALE)


def first_kernel(q_ref, bias_ref, *refs, takes, parts, heads, new_rows, span):
    *key_refs, acc_ref, high_ref, sum_ref, held_ref, own_ref, mark_ref, k_ref = refs
    all_of = functools.partial(all_rows, parts=parts)
    fill_keys(key_refs, takes, k_ref)
    share = own_ref.shape[0]
    first_own = pl.multiple_of(lax.axis_index("tp") * share, share)
    own_ref[...] = key_refs[0][pl.ds(first_own, share), :]
    mark_ref[...] = jnp.zeros_like(mark_ref)

    def scores_of(part):
        q = q_ref[tile_rows(part), :]
        held_ref[all_of(part), :] = q
        scores = product(q, k_ref[...], 1)
        first_row = (pl.program_id(0) * parts + part) * ROWS
        row = first_row + lax.broadcasted_iota(jnp.int32, (ROWS, new_rows), 0)
        key = lax.broadcasted_iota(jnp.int32, (ROWS, new_rows), 1)
        fresh = jnp.where(key * heads <= row, scores[:, :new_rows], MASKED)
        return jnp.concatenate([fresh, scores[:, new_rows:] + bias_ref[:, slice(*span)]], axis=1)

    def weights_of(part, scores):
        highest = row_highest(scores)
        weights = weigh(scores, highest)
        high_ref[all_of(part), :] = highest
        sum_ref[all_of(part), :] = lane_sums(weights)
        return (weights.astype(jnp.bfloat16),)

    def finish(part, weights):
        acc_ref[all_of(part), :] = product(weights, k_ref[...], 0)

    pipelined(parts, scores_of, weights_of, finish)


def next_kernel(held_ref, bias_ref, acc_in, high_in, sum_in, *refs, takes, parts, span, last, marks):
    all_of = functools.partial(all_rows, parts=parts)
    refs = refs[marks:]
    if last:
        *key_refs, out_ref, k_ref = refs
    else:
        *key_refs, acc_ref, high_ref, sum_ref, mark_ref, k_ref = refs
        mark_ref[...] = jnp.zeros_like(mark_ref)
    fill_keys(key_refs, takes, k_ref)
    wide = k_ref.shape[1] // LANES

    def scores_of(part):
        scores = product(held_ref[all_of(part), :], k_ref[...], 1)
        return scores + bias_ref[:, slice(*span)]

    def weights_of(part, scores):
        before = high_in[all_of(part), :]
        highest = jnp.maximum(before, row_highest(scores))
        kept = jnp.exp2((before - highest) * EXPONENT_SCALE)
        weights = weigh(scores, highest)
        totals = sum_in[all_of(part), :] * kept + lane_sums(weights)
        if last:
            totals = jnp.broadcast_to(jnp.sum(totals, axis=1, keepdims=True), (ROWS, LANES))
        else:
            high_ref[all_of(part), :] = highest
            sum_ref[all_of(part), :] = totals
        return weights.astype(jnp.bfloat16), kept, totals

    def finish(part, weights, kept, totals):
        accumulated = acc_in[all_of(part), :] * across(kept, wide)
        accumulated = accumulated + product(weights, k_ref[...], 0)
        if last:
            share = across(1.0 / totals, wide)
            out_ref[tile_rows(part), :] = (accumulated * share).astype(jnp.bfloat16)
        else:
            acc_ref[all_of(part), :] = accumulated

    pipelined(parts, scores_of, weights_of, finish)


def sort_kernel(pool_ref, out_ref, sems):
    height = lax.axis_index("req") // PLANE
    sign = 1 - 2 * lax.axis_index("tp")
    moves = []
    for number, step in enumerate(STEPS):
        source = pool_ref.at[lax.rem(height + sign * step + RING, RING)]
        moves.append(pltpu.make_async_copy(source, out_ref.at[:, number], sems.at[number]))
    for move in moves:
        move.start()
    for move in moves:
        move.wait()


def whole(array):
    return pl.BlockSpec(array.shape, lambda i: (0,) * array.ndim)


def resident(array):
    return pltpu.with_memory_space_constraint(array, pltpu.VMEM)


RESIDENT = pl.BlockSpec(memory_space=pltpu.VMEM)


def sort_pages(pool):
    ring, plane, half_rows, width = pool.shape
    return pl.pallas_call(
        sort_kernel,
        in_specs=[pl.BlockSpec(memory_space=pl.ANY)],
        out_specs=RESIDENT,
        out_shape=pltpu.VMEM((plane, ring, half_rows, width), pool.dtype),
        scratch_shapes=[pltpu.SemaphoreType.DMA((ring,))],
        compiler_params=pltpu.CompilerParams(vmem_limit_bytes=VMEM_BYTES),
        name="sort_pages",
    )(pltpu.with_memory_space_constraint(pool, pltpu.HBM))


def attend(kernel, flat_q, keys, bias, state, mark, parts, out_specs, out_shape, aliases):
    rows, width = flat_q.shape
    takes = [(key[1:] if isinstance(key, tuple) else (0, key.shape[0])) for key in keys]
    keys = [key[0] if isinstance(key, tuple) else key for key in keys]
    key_count = sum(high - low for low, high in takes)
    q_spec = RESIDENT if state else row_tile(parts, width)
    q_space = pltpu.VMEM if state else pltpu.HBM
    return pl.pallas_call(
        functools.partial(kernel, takes=takes, parts=parts),
        grid=(rows // (ROWS * parts),),
        in_specs=[q_spec, whole(bias)]
        + [RESIDENT for _ in state]
        + [whole(part) for part in mark]
        + [RESIDENT for _ in keys],
        out_specs=out_specs,
        out_shape=out_shape,
        input_output_aliases=aliases,
        scratch_shapes=[pltpu.VMEM((key_count, width), jnp.bfloat16)],
        compiler_params=pltpu.CompilerParams(vmem_limit_bytes=VMEM_BYTES),
        cost_estimate=pl.CostEstimate(flops=0, bytes_accessed=1 << 16, transcendentals=0),
        name="attend",
    )(
        pltpu.with_memory_space_constraint(flat_q, q_space),
        bias,
        *[resident(part) for part in state],
        *mark,
        *[resident(key) for key in keys],
    )


def row_tile(parts, width):
    return pl.BlockSpec((ROWS * parts, width), lambda i: (i, 0))


def state_shapes(rows, width):
    shapes = [(rows, width), (rows, LANES), (rows, LANES)]
    return [pltpu.VMEM(shape, jnp.float32) for shape in shapes]


def attend_first(flat_q, keys, bias, span, heads):
    rows, width = flat_q.shape
    new_rows = keys[0].shape[0]
    small = [(new_rows // 2, width), (8, LANES)]
    return attend(
        functools.partial(first_kernel, heads=heads, new_rows=new_rows, span=span),
        flat_q,
        keys,
        bias,
        [],
        [],
        FIRST_PARTS,
        [RESIDENT] * 4 + [pl.BlockSpec(shape, lambda i: (0, 0)) for shape in small],
        state_shapes(rows, width)
        + [
            pltpu.VMEM((rows, width), jnp.bfloat16),
            jax.ShapeDtypeStruct(small[0], jnp.bfloat16),
            jax.ShapeDtypeStruct(small[1], jnp.float32),
        ],
        {},
    )


def attend_next(held, keys, bias, span, state, mark, last):
    rows, width = held.shape
    kernel = functools.partial(next_kernel, span=span, last=last, marks=len(mark))
    if last:
        out = row_tile(LAST_PARTS, width), jax.ShapeDtypeStruct((rows, width), jnp.bfloat16)
        return attend(kernel, held, keys, bias, state, mark, LAST_PARTS, *out, {})
    specs = [RESIDENT] * 3 + [pl.BlockSpec((8, LANES), lambda i: (0, 0))]
    shapes = state_shapes(rows, width) + [jax.ShapeDtypeStruct((8, LANES), jnp.float32)]
    aliases = {2: 0, 3: 1, 4: 2}
    return attend(kernel, held, keys, bias, state, mark, NEXT_PARTS, specs, shapes, aliases)


def along_ring(blocks, step):
    pairs = []
    for z in range(RING):
        for place in range(PLANE):
            for core, distance in ((0, step), (1, -step)):
                target = ((z + distance) % RING) * PLANE + place
                pairs.append(((z * PLANE + place) * 2 + core, target * 2 + core))
    return lax.ppermute(blocks, ("req", "tp"), pairs)


def body(stretch_states, w_down, latent_gain, queries, page_pool, page_table, prefix_len):
    side = lax.axis_index("tp")
    sign = 1 - 2 * side
    height = lax.axis_index("req") // PLANE
    half_rows, width = page_pool.shape[2:]
    pool = page_pool[0].reshape(RING, PLANE, half_rows, width)

    by_place = sort_pages(pool)
    by_place, page_table, stretch_states = lax.optimization_barrier(
        (by_place, page_table, stretch_states)
    )
    planes = [[z * PLANE + place for place in range(PLANE)] for z in range(RING)]
    crossed = lax.all_to_all(
        by_place, "req", split_axis=0, concat_axis=0, axis_index_groups=planes, tiled=True
    )
    partial_value = jnp.dot(stretch_states[0], w_down, preferred_element_type=jnp.float32)
    summed = partial_value + lax.ppermute(partial_value, "tp", SWAP)
    latents = normalize(summed, latent_gain)
    new_rows = latents.shape[0]

    place = jnp.arange(RING * PLANE, dtype=jnp.int32)
    logical = jnp.sum(
        jnp.where(page_table[0][None, :] == place[:, None], place[None, :], 0), axis=1
    ).reshape(RING, PLANE)
    steps = jnp.array([step for step, _ in BLOCKS], dtype=jnp.int32)
    others = jnp.array([other for _, other in BLOCKS], dtype=jnp.int32)
    page = jnp.take(logical, (height - sign * steps) % RING, axis=0)
    half = (side + others) % 2
    token = page[:, :, None] * (2 * half_rows) + (half * half_rows)[:, None, None]
    token = token + jnp.arange(half_rows, dtype=jnp.int32)
    bias = jnp.where(token.reshape(1, -1) < prefix_len[0], 0.0, MASKED).astype(jnp.float32)

    crossed, latents, bias = lax.optimization_barrier((crossed, latents, bias))
    handed = lax.ppermute(
        jnp.stack([crossed[:, 5], crossed[:, 6], crossed[:, 7], crossed[:, 0]]), "tp", SWAP
    )
    heads = queries.shape[2]
    flat_q = queries[0].reshape(new_rows * heads, width)
    span = lambda phase: tuple(edge * PLANE * half_rows for edge in PHASES[phase])
    block_rows = PLANE * half_rows
    flat = lambda block: block.reshape(-1, width)
    both = lambda block: [flat(block), flat(lax.ppermute(block, "tp", SWAP))]

    one = along_ring(jnp.stack([crossed[:, FORWARD[1]], handed[0], crossed[:, 1]]), 1)
    two = along_ring(jnp.stack([crossed[:, FORWARD[2]], handed[1]]), 2)
    keys = [latents, flat(crossed[:, 0]), (flat(handed), 3 * block_rows, 4 * block_rows)]
    *state, held, own_rows, mark = attend_first(flat_q, keys, bias, span(0), heads)

    one, mark = lax.optimization_barrier((one, mark))
    three = along_ring(jnp.stack([crossed[:, FORWARD[3]], handed[2], one[2]]), 3)
    two, mark = lax.optimization_barrier((two, mark))
    two = both(two)
    keys = [(key, 0, 2 * block_rows) for key in both(one)]
    *state, mark = attend_next(held, keys, bias, span(1), state, [mark], False)
    *state, mark = attend_next(held, two, bias, span(2), state, [mark], False)
    three, mark = lax.optimization_barrier((three, mark))
    attended = attend_next(held, both(three), bias, span(3), state, [mark], True)
    return (own_rows[None], attended.reshape(1, new_rows, heads, width))


def solution(mesh):
    return jax.shard_map(
        body,
        mesh=mesh,
        in_specs=(
            P("req", None, "tp"),
            P("tp", None),
            P(),
            P("req", None, "tp", None),
            P("req", None, "tp", None),
            P("req", None),
            P("req"),
        ),
        out_specs=(P("req", "tp", None), P("req", None, "tp", None)),
        check_vma=False,
    )
```
